32 devices in a mesh: gx: 8 (over z, y), gy: 4 (over x, core).
Axes of the slice: x: 2, y: 2, z: 4, core: 2. Of those that a mesh axis runs over, the one named last changes fastest.
Arguments:
- tracers: float32 [10, 4, 256, 1024], P(None, None, 'gy', 'gx'), may hold values from -3.4 to 3.4
- kappa: float32 [4, 256, 1024], P(None, 'gy', 'gx'), may hold values from 0.00098 to 8
Outputs:
- diffused: float32 [10, 4, 256, 1024], P(None, None, 'gy', 'gx')
The draws below stay inside these ranges and needn't reach their ends.
All inputs are finite; a program needn't handle non-finite values.
Results may differ from the reference program's by a relative error of at most 0.00055.
Values sent between devices are 32-bit elements; how exact they have to be, the bound alone decides.
A program may use at most 64 MiB of HBM per device.

```python
import math
import jax
import jax.numpy as jnp
from jax import lax

TRACERS = 10
NZ = 4
NX = 1024
NY = 256


def draw_tracers(key, part):
    keys = jax.random.split(jax.random.fold_in(key, 11), 5)
    shape = (TRACERS, NZ, NY, NX)
    xpos = lax.broadcasted_iota(jnp.float32, (1, 1, 1, NX), 3) / NX
    ypos = (lax.broadcasted_iota(jnp.float32, (1, 1, NY, 1), 2) + 0.5) / NY
    mode_x = jax.random.randint(keys[0], (TRACERS, NZ, 1, 1), 1, 4).astype(jnp.float32)
    mode_y = jax.random.randint(keys[1], (TRACERS, NZ, 1, 1), 1, 3).astype(jnp.float32)
    phase = jax.random.uniform(keys[2], (TRACERS, NZ, 1, 1), jnp.float32, 0.0, 2.0 * math.pi)
    amplitude = jax.random.uniform(keys[3], (TRACERS, NZ, 1, 1), jnp.float32, 0.5, 1.0)
    smooth = amplitude * jnp.sin(2.0 * math.pi * mode_x * xpos + phase) * jnp.sin(math.pi * mode_y * ypos)
    rough = 0.6 * jnp.clip(jax.random.normal(keys[4], shape, jnp.float32), -4.0, 4.0)
    return (smooth + rough).astype(jnp.float32)


def kappa_field(large, cells, smooth_share, rough_share):
    weight_field = smooth_share * (1.0 + large) + rough_share * cells
    return 8.0 * jnp.exp(-9.0 * weight_field)


def draw_kappa(key, part):
    keys = jax.random.split(jax.random.fold_in(key, 23), 5)
    shape = (NZ, NY, NX)
    xpos = lax.broadcasted_iota(jnp.float32, (1, 1, NX), 2) / NX
    ypos = lax.broadcasted_iota(jnp.float32, (1, NY, 1), 1) / NY
    mode_x = jax.random.randint(keys[0], (NZ, 1, 1), 1, 4).astype(jnp.float32)
    mode_y = jax.random.randint(keys[1], (NZ, 1, 1), 1, 3).astype(jnp.float32)
    phase_x = jax.random.uniform(keys[2], (NZ, 1, 1), jnp.float32, 0.0, 2.0 * math.pi)
    phase_y = jax.random.uniform(keys[3], (NZ, 1, 1), jnp.float32, 0.0, 2.0 * math.pi)
    large = jnp.sin(2.0 * math.pi * mode_x * xpos + phase_x) * jnp.cos(2.0 * math.pi * mode_y * ypos + phase_y)
    cells = jax.random.uniform(keys[4], shape, jnp.float32, 0.0, 1.0)
    return kappa_field(large, cells, 0.35, 0.3).astype(jnp.float32)


def setup_inputs(seed: int = 0) -> dict:
    key_list = jax.random.split(jax.random.key(seed), 3)
    tracers = draw_tracers(jax.random.fold_in(key_list[2], 71), 0)
    kappa = draw_kappa(jax.random.fold_in(key_list[2], 71), 0)
    return dict(tracers=tracers, kappa=kappa)


RATE = 20000.0
RATE_Z = 0.05


def vertical(field, faces):
    flux = faces * (field[1:] - field[:-1])
    zeros_plane = jnp.zeros_like(field[:1])
    return field + RATE_Z * (jnp.concatenate([flux, zeros_plane], 0) - jnp.concatenate([zeros_plane, flux], 0))


def factorize(lower, diagonal, upper):
    def advance(carry, items):
        low_value, diag_value, up_value = items
        pivot = diag_value - low_value * carry
        ratio = up_value / pivot
        return ratio, (ratio, pivot)

    start_ratio = jnp.zeros(lower.shape[1:], lower.dtype)
    final_ratio, (ratios, pivots) = lax.scan(advance, start_ratio, (lower, diagonal, upper))
    return ratios, pivots


def thomas_sweep(lower, ratios, pivots, right):
    def forward(carry, items):
        low_value, pivot, value = items
        result = (value - low_value * carry) / pivot
        return result, result

    zeros_line = jnp.zeros(right.shape[1:], right.dtype)
    final_forward, eliminated = lax.scan(forward, zeros_line, (lower, pivots, right))

    def backward(carry, items):
        ratio, value = items
        result = value - ratio * carry
        return result, result

    final_back, solved = lax.scan(backward, zeros_line, (ratios, eliminated), reverse=True)
    return solved


def cyclic_parts(lower, diagonal, upper):
    length = diagonal.shape[0]
    shift_value = -diagonal[0]
    corner_low = lower[0]
    corner_up = upper[length - 1]
    modified = diagonal.at[0].set(diagonal[0] - shift_value)
    modified = modified.at[length - 1].set(diagonal[length - 1] - corner_low * corner_up / shift_value)
    ratios, pivots = factorize(lower, modified, upper)
    helper = jnp.zeros_like(diagonal).at[0].set(shift_value).at[length - 1].set(corner_up)
    spike = thomas_sweep(lower, ratios, pivots, helper)
    return ratios, pivots, spike, shift_value, corner_low


def cyclic_solve(parts, lower, right):
    ratios, pivots, spike, shift_value, corner_low = parts
    length = right.shape[0]
    base = thomas_sweep(lower, ratios, pivots, right)
    weight = (base[0] + corner_low * base[length - 1] / shift_value) / (
        1.0 + spike[0] + corner_low * spike[length - 1] / shift_value)
    return base - weight * spike


def reference(tracers, kappa):
    east_face = 0.5 * (kappa + jnp.roll(kappa, -1, 2))
    west_face = jnp.roll(east_face, 1, 2)
    row_index = lax.broadcasted_iota(jnp.int32, kappa.shape, 1)
    north_face = jnp.where(row_index == NY - 1, 0.0, 0.5 * (kappa + jnp.roll(kappa, -1, 1)))
    south_face = jnp.roll(north_face, 1, 1)
    vertical_faces = 0.5 * (kappa[:-1] + kappa[1:])
    lower_x = jnp.moveaxis(-RATE * west_face, 2, 0)
    diag_x = jnp.moveaxis(1.0 + RATE * (west_face + east_face), 2, 0)
    upper_x = jnp.moveaxis(-RATE * east_face, 2, 0)
    parts_x = cyclic_parts(lower_x, diag_x, upper_x)
    lower_y = jnp.moveaxis(-RATE * south_face, 1, 0)
    diag_y = jnp.moveaxis(1.0 + RATE * (south_face + north_face), 1, 0)
    upper_y = jnp.moveaxis(-RATE * north_face, 1, 0)
    ratios_y, pivots_y = factorize(lower_y, diag_y, upper_y)

    def one_tracer(field):
        start_field = vertical(field, vertical_faces)
        across = jnp.moveaxis(cyclic_solve(parts_x, lower_x, jnp.moveaxis(start_field, 2, 0)), 0, 2)
        solved = thomas_sweep(lower_y, ratios_y, pivots_y, jnp.moveaxis(across, 1, 0))
        return jnp.moveaxis(solved, 0, 1)

    return lax.map(one_tracer, tracers)
```

```python
import functools

import jax
import jax.numpy as jnp
from jax import lax
from jax.experimental import pallas as pl
from jax.experimental.pallas import tpu as pltpu
from jax.sharding import PartitionSpec as P

RATE = 20000.0
RATE_Z = 0.05
SUB = 8
HALF = 0.5 * RATE


def merge(left, right):
    g_l, ef_l, el_l, kf_l, kl_l = left
    g_r, ef_r, el_r, kf_r, kl_r = right
    face = HALF * (kl_l + kf_r)
    e_p = el_l + g_l
    e_q = ef_r + g_r
    inverse = 1.0 / (e_p * e_q + face * (e_p + e_q))
    a_pp = (e_q + face) * inverse
    a_pq = face * inverse
    a_qq = (e_p + face) * inverse
    chain = (
        g_l * a_pq * g_r,
        ef_l + g_l * (el_l * a_pp + a_pq * ef_r),
        el_r + g_r * (ef_r * a_qq + a_pq * el_l),
        kf_l,
        kl_r,
    )
    return chain, (a_pp, a_pq, a_qq, g_l, g_r)


def middle(inverse, high):
    a_pp, a_pq, a_qq, g_l, g_r = inverse
    by_first = jnp.where(high, a_pq, a_pp) * g_l
    by_last = jnp.where(high, a_qq, a_pq) * g_r
    return by_first, by_last


def join_right(inverse, f_l, l_l, f_r, l_r):
    a_pp, a_pq, a_qq, g_l, g_r = inverse
    u = a_pp * l_l + a_pq * f_r
    v = a_pq * l_l + a_qq * f_r
    return f_l + g_l * u, l_r + g_r * v, u, v


def sublane_pair(value, level, high, axis):
    step = 1 << level
    low_side = jnp.where(high, pltpu.roll(value, step, axis), value)
    high_side = jnp.where(high, value, pltpu.roll(value, SUB - step, axis))
    return low_side, high_side


def high_bit(shape, axis, level):
    return (lax.broadcasted_iota(jnp.int32, shape, axis) & (1 << level)) != 0


def factor(kappa, cells, levels, message, tracers):
    planes, length = kappa.shape[0], kappa.shape[1]
    group = length // SUB
    k = [kappa[:, pl.ds(i, SUB, stride=group), :] for i in range(group)]
    coupling = HALF * (k[0] + k[1])
    first = jnp.ones_like(coupling)
    last = jnp.ones_like(coupling)
    for j in range(1, group - 1):
        face = HALF * (k[j] + k[j + 1])
        inverse = 1.0 / (last + coupling + face)
        to_first = coupling * inverse
        to_next = face * inverse
        cells[j, 0] = to_first
        cells[j, 1] = to_next
        cells[j, 2] = inverse
        first = first + to_first * last
        last = 1.0 + to_next * last
        coupling = coupling * to_next
    chain = (coupling, first, last, k[0], k[group - 1])
    for level in range(3):
        high = high_bit(coupling.shape, 1, level)
        pairs = [sublane_pair(value, level, high, 1) for value in chain]
        chain, inverse = merge([a for a, b in pairs], [b for a, b in pairs])
        for i, value in enumerate(inverse + middle(inverse, high)):
            levels[level, i] = value
    for i, value in enumerate(chain):
        for plane in range(planes):
            message[0, 2 * tracers + i, pl.ds(plane, 1), :] = value[plane, 0:1, :]


def eliminate(field, plane, cells, levels, kept, kept_levels, message):
    tracers, length = field.shape[0], field.shape[2]
    group = length // SUB

    def row(i):
        return field[:, plane, pl.ds(i, SUB, stride=group), :]

    first, last = row(0), row(1)
    for j in range(1, group - 1):
        kept[j, :, plane] = last
        first = first + cells[j, 0, plane] * last
        last = row(j + 1) + cells[j, 1, plane] * last
    for level in range(3):
        high = high_bit(first.shape, 1, level)
        inverse = [levels[level, i, plane] for i in range(5)]
        f_l, f_r = sublane_pair(first, level, high, 1)
        l_l, l_r = sublane_pair(last, level, high, 1)
        first, last, u, v = join_right(inverse, f_l, l_l, f_r, l_r)
        kept_levels[level, :, plane] = jnp.where(high, v, u)
    message[0, 0:tracers, pl.ds(plane, 1), :] = first[:, 0:1, :]
    message[0, tracers : 2 * tracers, pl.ds(plane, 1), :] = last[:, 0:1, :]


def back(field, plane, cells, levels, kept, kept_levels, ends):
    tracers, length = field.shape[0], field.shape[2]
    group = length // SUB
    shape = (tracers, SUB, field.shape[3])
    first = jnp.broadcast_to(ends[0:tracers, pl.ds(plane, 1), :], shape)
    last = jnp.broadcast_to(ends[tracers : 2 * tracers, pl.ds(plane, 1), :], shape)
    for level in reversed(range(3)):
        high = high_bit(shape, 1, level)
        inner = (
            kept_levels[level, :, plane]
            + levels[level, 5, plane] * first
            + levels[level, 6, plane] * last
        )
        first = jnp.where(high, inner, first)
        last = jnp.where(high, last, inner)
    field[:, plane, pl.ds(0, SUB, stride=group), :] = first
    field[:, plane, pl.ds(group - 1, SUB, stride=group), :] = last
    for j in reversed(range(1, group - 1)):
        last = (
            cells[j, 2, plane] * kept[j, :, plane]
            + cells[j, 0, plane] * first
            + cells[j, 1, plane] * last
        )
        field[:, plane, pl.ds(j, SUB, stride=group), :] = last


def partner(index, level):
    step = 1 << level
    return index + step - 2 * step * ((index // step) % 2)


def exchange(sizes, axis, message, received, ends, send_sems, recv_sems, cyclic):
    tracers = ends.shape[0] // 2
    index = {name: lax.axis_index(name) for name in sizes}
    me = index[axis]
    steps = []
    own = None
    for level in range(sizes[axis].bit_length() - 1):
        target = dict(index)
        target[axis] = partner(me, level)
        copy = pltpu.make_async_remote_copy(
            src_ref=message.at[level],
            dst_ref=received.at[level],
            send_sem=send_sems.at[level],
            recv_sem=recv_sems.at[level],
            device_id=tuple(target[name] for name in sizes),
            device_id_type=pl.DeviceIdType.MESH,
        )
        copy.start()
        high = (me // (1 << level)) % 2 == 1
        copy.wait()
        mine, other = message[level], received[level]
        left = jnp.where(high, other, mine)
        right = jnp.where(high, mine, other)
        chain, inverse = merge(
            [left[2 * tracers + i] for i in range(5)], [right[2 * tracers + i] for i in range(5)]
        )
        first, last, u, v = join_right(
            inverse,
            left[0:tracers],
            left[tracers : 2 * tracers],
            right[0:tracers],
            right[tracers : 2 * tracers],
        )
        steps.append((high, jnp.where(high, v, u)) + middle(inverse, high))
        own = (chain, first, last)
        if level + 1 < message.shape[0]:
            message[level + 1, 0:tracers] = first
            message[level + 1, tracers : 2 * tracers] = last
            for i in range(5):
                message[level + 1, 2 * tracers + i] = chain[i]
    (coupling, e_first, e_last, k_first, k_last), first, last = own
    if cyclic:
        coupling = coupling + HALF * (k_last + k_first)
    inverse = 1.0 / (e_first * e_last + coupling * (e_first + e_last))
    both = coupling * inverse
    first, last = (
        (e_last + coupling) * inverse * first + both * last,
        both * first + (e_first + coupling) * inverse * last,
    )
    for high, inner, by_first, by_last in reversed(steps):
        inner = inner + by_first * first + by_last * last
        first = jnp.where(high, inner, first)
        last = jnp.where(high, last, inner)
    ends[0:tracers] = first
    ends[tracers : 2 * tracers] = last


def kernel(
    sizes,
    tracers_ref,
    kappa_ref,
    out_ref,
    x_field,
    x_kappa,
    x_cells,
    x_levels,
    x_kept,
    x_kept_levels,
    x_message,
    x_received,
    x_ends,
    y_cells,
    y_levels,
    y_kept,
    y_kept_levels,
    y_message,
    y_received,
    y_ends,
    x_send,
    x_recv,
    y_send,
    y_recv,
):
    tracers, planes, rows, columns = tracers_ref.shape
    pairs = tracers // 2
    index = {name: lax.axis_index(name) for name in sizes}
    barrier = pltpu.get_barrier_semaphore()
    partners = 0
    for axis in sizes:
        for level in range(sizes[axis].bit_length() - 1):
            target = dict(index)
            target[axis] = partner(index[axis], level)
            pl.semaphore_signal(
                barrier,
                inc=1,
                device_id=tuple(target[name] for name in sizes),
                device_id_type=pl.DeviceIdType.MESH,
            )
            partners += 1

    for plane in range(planes):
        block = kappa_ref[plane]
        x_kappa[plane] = jnp.concatenate([block, block], 0).T
    factor(x_kappa, x_cells, x_levels, x_message, pairs)
    factor(kappa_ref, y_cells, y_levels, y_message, tracers)

    faces = [0.5 * RATE_Z * (kappa_ref[z] + kappa_ref[z + 1]) for z in range(planes - 1)]

    def load_pair(pair, carry):
        fields = [
            tracers_ref[pl.ds(2 * pair, 2), z].reshape(2 * rows, columns) for z in range(planes)
        ]
        flux = [
            jnp.concatenate([faces[z], faces[z]], 0) * (fields[z + 1] - fields[z])
            for z in range(planes - 1)
        ]
        for z in range(planes):
            start = fields[z]
            if z < planes - 1:
                start = start + flux[z]
            if z > 0:
                start = start - flux[z - 1]
            x_field[pair, z] = start.T
        return carry

    lax.fori_loop(0, pairs, load_pair, 0)

    def eliminate_x(plane, carry):
        eliminate(x_field, plane, x_cells, x_levels, x_kept, x_kept_levels, x_message)
        return carry

    for plane in range(planes):
        eliminate_x(plane, 0)
    pl.semaphore_wait(barrier, partners)
    exchange(sizes, "gx", x_message, x_received, x_ends, x_send, x_recv, True)
    for plane in range(planes):
        back(x_field, plane, x_cells, x_levels, x_kept, x_kept_levels, x_ends)

    def turn_pair(pair, carry):
        for z in range(planes):
            out_ref[pl.ds(2 * pair, 2), z] = x_field[pair, z].T.reshape(2, rows, columns)
        return carry

    lax.fori_loop(0, pairs, turn_pair, 0)
    for plane in range(planes):
        eliminate(out_ref, plane, y_cells, y_levels, y_kept, y_kept_levels, y_message)
    exchange(sizes, "gy", y_message, y_received, y_ends, y_send, y_recv, False)
    for plane in range(planes):
        back(out_ref, plane, y_cells, y_levels, y_kept, y_kept_levels, y_ends)


def shards(sizes, tracers, kappa):
    count, planes, rows, columns = tracers.shape
    pairs = count // 2
    lanes = 2 * rows

    def scratch(*shape):
        return pltpu.VMEM(shape, jnp.float32)

    def line(fields, length, width, axis):
        group = length // SUB
        hops = sizes[axis].bit_length() - 1
        message = (hops, 2 * fields + 5, planes, width)
        return [
            scratch(group, 3, planes, SUB, width),
            scratch(3, 7, planes, SUB, width),
            scratch(group, fields, planes, SUB, width),
            scratch(3, fields, planes, SUB, width),
            scratch(*message),
            scratch(*message),
            scratch(2 * fields, planes, width),
        ]

    hops_x = sizes["gx"].bit_length() - 1
    hops_y = sizes["gy"].bit_length() - 1
    return pl.pallas_call(
        functools.partial(kernel, sizes),
        out_shape=jax.ShapeDtypeStruct(tracers.shape, jnp.float32),
        in_specs=[pl.BlockSpec(memory_space=pltpu.VMEM)] * 2,
        out_specs=pl.BlockSpec(memory_space=pltpu.VMEM),
        scratch_shapes=[scratch(pairs, planes, columns, lanes), scratch(planes, columns, lanes)]
        + line(pairs, columns, lanes, "gx")
        + line(count, rows, columns, "gy")
        + [pltpu.SemaphoreType.DMA((hops,)) for hops in (hops_x, hops_x, hops_y, hops_y)],
        compiler_params=pltpu.CompilerParams(
            collective_id=0, has_side_effects=True, vmem_limit_bytes=40 * 1024 * 1024
        ),
    )(tracers, kappa)


def solution(mesh):
    sizes = {name: mesh.shape[name] for name in ("gx", "gy")}
    placed = (P(None, None, "gy", "gx"), P(None, "gy", "gx"))
    return jax.shard_map(
        functools.partial(shards, sizes),
        mesh=mesh,
        in_specs=placed,
        out_specs=P(None, None, "gy", "gx"),
        check_vma=False,
    )
```

```python
import functools

import jax
import jax.numpy as jnp
from jax import lax
from jax.experimental import pallas as pl
from jax.experimental.pallas import tpu as pltpu
from jax.sharding import PartitionSpec as P

RATE = 20000.0
RATE_Z = 0.05
SUB = 8
HALF = 0.5 * RATE


def merge(left, right):
    g_l, ef_l, el_l, kf_l, kl_l = left
    g_r, ef_r, el_r, kf_r, kl_r = right
    face = HALF * (kl_l + kf_r)
    e_p = el_l + g_l
    e_q = ef_r + g_r
    inverse = 1.0 / (e_p * e_q + face * (e_p + e_q))
    a_pp = (e_q + face) * inverse
    a_pq = face * inverse
    a_qq = (e_p + face) * inverse
    chain = (
        g_l * a_pq * g_r,
        ef_l + g_l * (el_l * a_pp + a_pq * ef_r),
        el_r + g_r * (ef_r * a_qq + a_pq * el_l),
        kf_l,
        kl_r,
    )
    return chain, (a_pp, a_pq, a_qq, g_l, g_r)


def middle(inverse, high):
    a_pp, a_pq, a_qq, g_l, g_r = inverse
    by_first = jnp.where(high, a_pq, a_pp) * g_l
    by_last = jnp.where(high, a_qq, a_pq) * g_r
    return by_first, by_last


def join_right(inverse, f_l, l_l, f_r, l_r):
    a_pp, a_pq, a_qq, g_l, g_r = inverse
    u = a_pp * l_l + a_pq * f_r
    v = a_pq * l_l + a_qq * f_r
    return f_l + g_l * u, l_r + g_r * v, u, v


def sublane_pair(value, level, high, axis):
    step = 1 << level
    low_side = jnp.where(high, pltpu.roll(value, step, axis), value)
    high_side = jnp.where(high, value, pltpu.roll(value, SUB - step, axis))
    return low_side, high_side


def high_bit(shape, axis, level):
    return (lax.broadcasted_iota(jnp.int32, shape, axis) & (1 << level)) != 0


def factor(kappa, cells, levels, message):
    planes, length = kappa.shape[0], kappa.shape[1]
    group = length // SUB
    k = [kappa[:, pl.ds(i, SUB, stride=group), :] for i in range(group)]
    coupling = HALF * (k[0] + k[1])
    first = jnp.ones_like(coupling)
    last = jnp.ones_like(coupling)
    for j in range(1, group - 1):
        face = HALF * (k[j] + k[j + 1])
        inverse = 1.0 / (last + coupling + face)
        to_first = coupling * inverse
        to_next = face * inverse
        cells[j, 0] = to_first
        cells[j, 1] = to_next
        cells[j, 2] = inverse
        first = first + to_first * last
        last = 1.0 + to_next * last
        coupling = coupling * to_next
    chain = (coupling, first, last, k[0], k[group - 1])
    for level in range(3):
        high = high_bit(coupling.shape, 1, level)
        pairs = [sublane_pair(value, level, high, 1) for value in chain]
        chain, inverse = merge([a for a, b in pairs], [b for a, b in pairs])
        for i, value in enumerate(inverse + middle(inverse, high)):
            levels[level, i] = value
    for i, value in enumerate(chain):
        for plane in range(planes):
            message[0, i, pl.ds(plane, 1), :] = value[plane, 0:1, :]


def eliminate(field, part, plane, cells, levels, kept, kept_levels, message):
    start, count = part
    group = field.shape[2] // SUB
    fields = pl.ds(start, count)

    def row(i):
        return field[fields, plane, pl.ds(i, SUB, stride=group), :]

    first, last = row(0), row(1)
    for j in range(1, group - 1):
        kept[j, fields, plane] = last
        first = first + cells[j, 0, plane] * last
        last = row(j + 1) + cells[j, 1, plane] * last
    for level in range(3):
        high = high_bit(first.shape, 1, level)
        inverse = [levels[level, i, plane] for i in range(5)]
        f_l, f_r = sublane_pair(first, level, high, 1)
        l_l, l_r = sublane_pair(last, level, high, 1)
        first, last, u, v = join_right(inverse, f_l, l_l, f_r, l_r)
        kept_levels[level, fields, plane] = jnp.where(high, v, u)
    message[0, 0:count, pl.ds(plane, 1), :] = first[:, 0:1, :]
    message[0, count : 2 * count, pl.ds(plane, 1), :] = last[:, 0:1, :]


def back(field, part, plane, cells, levels, kept, kept_levels, ends):
    start, count = part
    group = field.shape[2] // SUB
    fields = pl.ds(start, count)
    shape = (count, SUB, field.shape[3])
    first = jnp.broadcast_to(ends[0:count, pl.ds(plane, 1), :], shape)
    last = jnp.broadcast_to(ends[count : 2 * count, pl.ds(plane, 1), :], shape)
    for level in reversed(range(3)):
        high = high_bit(shape, 1, level)
        inner = (
            kept_levels[level, fields, plane]
            + levels[level, 5, plane] * first
            + levels[level, 6, plane] * last
        )
        first = jnp.where(high, inner, first)
        last = jnp.where(high, last, inner)
    field[fields, plane, pl.ds(0, SUB, stride=group), :] = first
    field[fields, plane, pl.ds(group - 1, SUB, stride=group), :] = last
    for j in reversed(range(1, group - 1)):
        last = (
            cells[j, 2, plane] * kept[j, fields, plane]
            + cells[j, 0, plane] * first
            + cells[j, 1, plane] * last
        )
        field[fields, plane, pl.ds(j, SUB, stride=group), :] = last


def flipped(index, bits):
    level = 0
    target = index
    while (1 << level) <= bits:
        step = 1 << level
        if bits & step:
            target = target + step - 2 * step * ((index // step) % 2)
        level += 1
    return target


def device(sizes, axis, bits):
    index = {name: lax.axis_index(name) for name in sizes}
    index[axis] = flipped(index[axis], bits)
    return tuple(index[name] for name in sizes)


def send(sizes, axis, buffer, send_sems, recv_sems, row):
    copies = []
    for bits in range(1, sizes[axis]):
        copy = pltpu.make_async_remote_copy(
            src_ref=buffer.at[0],
            dst_ref=buffer.at[bits],
            send_sem=send_sems.at[row, bits],
            recv_sem=recv_sems.at[row, bits],
            device_id=device(sizes, axis, bits),
            device_id_type=pl.DeviceIdType.MESH,
        )
        copy.start()
        copies.append(copy)
    return copies


def halves(value, high):
    value = value.reshape((value.shape[0] // 2, 2) + value.shape[1:])
    even, odd = value[:, 0], value[:, 1]
    return jnp.where(high, odd, even), jnp.where(high, even, odd)


def join_coefficients(sizes, axis, buffer, cyclic):
    me = lax.axis_index(axis)
    chain = [buffer[:, i] for i in range(5)]
    steps = []
    for level in range(sizes[axis].bit_length() - 1):
        high = (me // (1 << level)) % 2 == 1
        pairs = [halves(value, high) for value in chain]
        chain, inverse = merge([a for a, b in pairs], [b for a, b in pairs])
        steps.append((high, inverse, middle([value[0] for value in inverse], high)))
    coupling, e_first, e_last, k_first, k_last = [value[0] for value in chain]
    if cyclic:
        coupling = coupling + HALF * (k_last + k_first)
    inverse = 1.0 / (e_first * e_last + coupling * (e_first + e_last))
    closing = (
        (e_last + coupling) * inverse,
        coupling * inverse,
        (e_first + coupling) * inverse,
    )
    return steps, closing


def find_ends(joined, buffer, ends):
    steps, closing = joined
    count = ends.shape[0] // 2
    first, last = buffer[:, 0:count], buffer[:, count : 2 * count]
    inner_parts = []
    for high, inverse, weights in steps:
        f_l, f_r = halves(first, high)
        l_l, l_r = halves(last, high)
        first, last, u, v = join_right([value[:, None] for value in inverse], f_l, l_l, f_r, l_r)
        inner_parts.append(jnp.where(high, v[0], u[0]))
    first, last = first[0], last[0]
    first, last = (
        closing[0] * first + closing[1] * last,
        closing[1] * first + closing[2] * last,
    )
    for (high, inverse, weights), inner in reversed(list(zip(steps, inner_parts))):
        inner = inner + weights[0] * first + weights[1] * last
        first = jnp.where(high, inner, first)
        last = jnp.where(high, last, inner)
    ends[0:count] = first
    ends[count : 2 * count] = last


def kernel(sizes, parts, tracers_hbm, kappa_hbm, out_ref, *scratch):
    pieces = len(parts)
    tracers_ref, kappa_ref, x_field, x_kappa = scratch[:4]
    scratch = scratch[4:]
    x_cells, x_levels, x_kept, x_kept_levels, x_coef = scratch[:5]
    x_buffers, x_ends = scratch[5 : 5 + pieces], scratch[5 + pieces : 5 + 2 * pieces]
    scratch = scratch[5 + 2 * pieces :]
    y_cells, y_levels, y_kept, y_kept_levels, y_coef = scratch[:5]
    y_buffers, y_ends = scratch[5 : 5 + pieces], scratch[5 + pieces : 5 + 2 * pieces]
    x_send, x_recv, y_send, y_recv, in_sems = scratch[5 + 2 * pieces :]
    tracers, planes, rows, columns = tracers_ref.shape
    y_parts = [(2 * start, 2 * count) for start, count in parts]

    barrier = pltpu.get_barrier_semaphore()
    partners = 0
    for axis in sizes:
        for bits in reversed(range(1, sizes[axis])):
            pl.semaphore_signal(
                barrier,
                inc=1,
                device_id=device(sizes, axis, bits),
                device_id_type=pl.DeviceIdType.MESH,
            )
            partners += 1
    kappa_copy = pltpu.make_async_copy(kappa_hbm, kappa_ref, in_sems.at[pieces])
    kappa_copy.start()
    loads = []
    for piece, (start, count) in enumerate(y_parts):
        block = pl.ds(start, count)
        load = pltpu.make_async_copy(
            tracers_hbm.at[block], tracers_ref.at[block], in_sems.at[piece]
        )
        load.start()
        loads.append(load)

    kappa_copy.wait()
    for plane in range(planes):
        block = kappa_ref[plane]
        x_kappa[plane] = jnp.concatenate([block, block], 0).T
    factor(x_kappa, x_cells, x_levels, x_coef)
    factor(kappa_ref, y_cells, y_levels, y_coef)

    faces = [0.5 * RATE_Z * (kappa_ref[z] + kappa_ref[z + 1]) for z in range(planes - 1)]

    def load_pair(pair, carry):
        fields = [
            tracers_ref[pl.ds(2 * pair, 2), z].reshape(2 * rows, columns) for z in range(planes)
        ]
        flux = [
            jnp.concatenate([faces[z], faces[z]], 0) * (fields[z + 1] - fields[z])
            for z in range(planes - 1)
        ]
        for z in range(planes):
            start = fields[z]
            if z < planes - 1:
                start = start + flux[z]
            if z > 0:
                start = start - flux[z - 1]
            x_field[pair, z] = start.T
        return carry

    for piece, (start, count) in enumerate(parts):
        loads[piece].wait()
        lax.fori_loop(start, start + count, load_pair, 0)
        for plane in range(planes):
            eliminate(
                x_field,
                parts[piece],
                plane,
                x_cells,
                x_levels,
                x_kept,
                x_kept_levels,
                x_buffers[piece],
            )
    pl.semaphore_wait(barrier, partners)
    x_copies = [send(sizes, "gx", x_coef, x_send, x_recv, pieces)]
    for piece in range(pieces):
        x_copies.append(send(sizes, "gx", x_buffers[piece], x_send, x_recv, piece))
    y_copies = [send(sizes, "gy", y_coef, y_send, y_recv, pieces)]
    for copy in x_copies[0]:
        copy.wait()
    x_joined = join_coefficients(sizes, "gx", x_coef, True)
    for copy in y_copies[0]:
        copy.wait()
    y_joined = join_coefficients(sizes, "gy", y_coef, False)

    def turn_pair(pair, carry):
        for z in range(planes):
            out_ref[pl.ds(2 * pair, 2), z] = x_field[pair, z].T.reshape(2, rows, columns)
        return carry

    for piece, (start, count) in enumerate(parts):
        for copy in x_copies[piece + 1]:
            copy.wait()
        find_ends(x_joined, x_buffers[piece], x_ends[piece])
        for plane in range(planes):
            back(
                x_field,
                parts[piece],
                plane,
                x_cells,
                x_levels,
                x_kept,
                x_kept_levels,
                x_ends[piece],
            )
        lax.fori_loop(start, start + count, turn_pair, 0)
        for plane in range(planes):
            eliminate(
                out_ref,
                y_parts[piece],
                plane,
                y_cells,
                y_levels,
                y_kept,
                y_kept_levels,
                y_buffers[piece],
            )
        y_copies.append(send(sizes, "gy", y_buffers[piece], y_send, y_recv, piece))
    for piece in range(pieces):
        for copy in y_copies[piece + 1]:
            copy.wait()
        find_ends(y_joined, y_buffers[piece], y_ends[piece])
        for plane in range(planes):
            back(
                out_ref,
                y_parts[piece],
                plane,
                y_cells,
                y_levels,
                y_kept,
                y_kept_levels,
                y_ends[piece],
            )


def shards(sizes, tracers, kappa):
    count, planes, rows, columns = tracers.shape
    pairs = count // 2
    lanes = 2 * rows
    early = (pairs + 1) // 2
    parts = [(0, early), (early, pairs - early)]

    def scratch(*shape):
        return pltpu.VMEM(shape, jnp.float32)

    def line(each, length, width, axis):
        fields = each * pairs
        group = length // SUB
        size = sizes[axis]
        return (
            [
                scratch(group, 3, planes, SUB, width),
                scratch(3, 7, planes, SUB, width),
                scratch(group, fields, planes, SUB, width),
                scratch(3, fields, planes, SUB, width),
                scratch(size, 5, planes, width),
            ]
            + [scratch(size, 2 * each * number, planes, width) for _, number in parts]
            + [scratch(2 * each * number, planes, width) for _, number in parts]
        )

    semaphores = [
        pltpu.SemaphoreType.DMA((len(parts) + 1, sizes[axis])) for axis in ("gx", "gx", "gy", "gy")
    ]
    return pl.pallas_call(
        functools.partial(kernel, sizes, parts),
        out_shape=jax.ShapeDtypeStruct(tracers.shape, jnp.float32),
        in_specs=[pl.BlockSpec(memory_space=pltpu.HBM)] * 2,
        out_specs=pl.BlockSpec(memory_space=pltpu.VMEM),
        scratch_shapes=[
            scratch(*tracers.shape),
            scratch(*kappa.shape),
            scratch(pairs, planes, columns, lanes),
            scratch(planes, columns, lanes),
        ]
        + line(1, columns, lanes, "gx")
        + line(2, rows, columns, "gy")
        + semaphores
        + [pltpu.SemaphoreType.DMA((len(parts) + 1,))],
        compiler_params=pltpu.CompilerParams(
            collective_id=0, has_side_effects=True, vmem_limit_bytes=48 * 1024 * 1024
        ),
    )(tracers, kappa)


def solution(mesh):
    sizes = {name: mesh.shape[name] for name in ("gx", "gy")}
    placed = (P(None, None, "gy", "gx"), P(None, "gy", "gx"))
    return jax.shard_map(
        functools.partial(shards, sizes),
        mesh=mesh,
        in_specs=placed,
        out_specs=P(None, None, "gy", "gx"),
        check_vma=False,
    )
```

```python
import functools

import jax
import jax.numpy as jnp
from jax import lax
from jax.experimental import pallas as pl
from jax.experimental.pallas import tpu as pltpu
from jax.sharding import PartitionSpec as P

RATE = 20000.0
RATE_Z = 0.05
SUB = 8
HALF = 0.5 * RATE


def merge(left, right):
    g_l, ef_l, el_l, kf_l, kl_l = left
    g_r, ef_r, el_r, kf_r, kl_r = right
    face = HALF * (kl_l + kf_r)
    e_p = el_l + g_l
    e_q = ef_r + g_r
    inverse = 1.0 / (e_p * e_q + face * (e_p + e_q))
    a_pp = (e_q + face) * inverse
    a_pq = face * inverse
    a_qq = (e_p + face) * inverse
    chain = (
        g_l * a_pq * g_r,
        ef_l + g_l * (el_l * a_pp + a_pq * ef_r),
        el_r + g_r * (ef_r * a_qq + a_pq * el_l),
        kf_l,
        kl_r,
    )
    return chain, (a_pp, a_pq, a_qq, g_l, g_r)


def middle(inverse, high):
    a_pp, a_pq, a_qq, g_l, g_r = inverse
    by_first = jnp.where(high, a_pq, a_pp) * g_l
    by_last = jnp.where(high, a_qq, a_pq) * g_r
    return by_first, by_last


def join_right(inverse, f_l, l_l, f_r, l_r):
    a_pp, a_pq, a_qq, g_l, g_r = inverse
    u = a_pp * l_l + a_pq * f_r
    v = a_pq * l_l + a_qq * f_r
    return f_l + g_l * u, l_r + g_r * v, u, v


def sublane_pair(value, level, high, axis):
    step = 1 << level
    low_side = jnp.where(high, pltpu.roll(value, step, axis), value)
    high_side = jnp.where(high, value, pltpu.roll(value, SUB - step, axis))
    return low_side, high_side


def high_bit(shape, axis, level):
    return (lax.broadcasted_iota(jnp.int32, shape, axis) & (1 << level)) != 0


def factor(kappa, cells, levels, message):
    planes, length = kappa.shape[0], kappa.shape[1]
    group = length // SUB
    k = [kappa[:, pl.ds(i, SUB, stride=group), :] for i in range(group)]
    coupling = HALF * (k[0] + k[1])
    first = jnp.ones_like(coupling)
    last = jnp.ones_like(coupling)
    for j in range(1, group - 1):
        face = HALF * (k[j] + k[j + 1])
        inverse = 1.0 / (last + coupling + face)
        to_first = coupling * inverse
        to_next = face * inverse
        cells[j, 0] = to_first
        cells[j, 1] = to_next
        cells[j, 2] = inverse
        first = first + to_first * last
        last = 1.0 + to_next * last
        coupling = coupling * to_next
    chain = (coupling, first, last, k[0], k[group - 1])
    for level in range(3):
        high = high_bit(coupling.shape, 1, level)
        pairs = [sublane_pair(value, level, high, 1) for value in chain]
        chain, inverse = merge([a for a, b in pairs], [b for a, b in pairs])
        for i, value in enumerate(inverse + middle(inverse, high)):
            levels[level, i] = value
    for i, value in enumerate(chain):
        for plane in range(planes):
            message[0, i, pl.ds(plane, 1), :] = value[plane, 0:1, :]


def eliminate(field, part, plane, cells, levels, kept, kept_levels, message):
    start, count = part
    group = field.shape[2] // SUB
    fields = pl.ds(start, count)

    def row(i):
        return field[fields, plane, pl.ds(i, SUB, stride=group), :]

    first, last = row(0), row(1)
    for j in range(1, group - 1):
        kept[j, fields, plane] = last
        first = first + cells[j, 0, plane] * last
        last = row(j + 1) + cells[j, 1, plane] * last
    for level in range(3):
        high = high_bit(first.shape, 1, level)
        inverse = [levels[level, i, plane] for i in range(5)]
        f_l, f_r = sublane_pair(first, level, high, 1)
        l_l, l_r = sublane_pair(last, level, high, 1)
        first, last, u, v = join_right(inverse, f_l, l_l, f_r, l_r)
        kept_levels[level, fields, plane] = jnp.where(high, v, u)
    message[0, 0:count, pl.ds(plane, 1), :] = first[:, 0:1, :]
    message[0, count : 2 * count, pl.ds(plane, 1), :] = last[:, 0:1, :]


def back(field, part, plane, cells, levels, kept, kept_levels, ends):
    start, count = part
    group = field.shape[2] // SUB
    fields = pl.ds(start, count)
    shape = (count, SUB, field.shape[3])
    first = jnp.broadcast_to(ends[0:count, pl.ds(plane, 1), :], shape)
    last = jnp.broadcast_to(ends[count : 2 * count, pl.ds(plane, 1), :], shape)
    for level in reversed(range(3)):
        high = high_bit(shape, 1, level)
        inner = (
            kept_levels[level, fields, plane]
            + levels[level, 5, plane] * first
            + levels[level, 6, plane] * last
        )
        first = jnp.where(high, inner, first)
        last = jnp.where(high, last, inner)
    field[fields, plane, pl.ds(0, SUB, stride=group), :] = first
    field[fields, plane, pl.ds(group - 1, SUB, stride=group), :] = last
    for j in reversed(range(1, group - 1)):
        last = (
            cells[j, 2, plane] * kept[j, fields, plane]
            + cells[j, 0, plane] * first
            + cells[j, 1, plane] * last
        )
        field[fields, plane, pl.ds(j, SUB, stride=group), :] = last


def flipped(index, bits):
    level = 0
    target = index
    while (1 << level) <= bits:
        step = 1 << level
        if bits & step:
            target = target + step - 2 * step * ((index // step) % 2)
        level += 1
    return target


def device(sizes, axis, bits):
    index = {name: lax.axis_index(name) for name in sizes}
    index[axis] = flipped(index[axis], bits)
    return tuple(index[name] for name in sizes)


def send(sizes, axis, buffer, send_sems, recv_sems, row):
    copies = []
    for bits in range(1, sizes[axis]):
        copy = pltpu.make_async_remote_copy(
            src_ref=buffer.at[0],
            dst_ref=buffer.at[bits],
            send_sem=send_sems.at[row, bits],
            recv_sem=recv_sems.at[row, bits],
            device_id=device(sizes, axis, bits),
            device_id_type=pl.DeviceIdType.MESH,
        )
        copy.start()
        copies.append(copy)
    return copies


def halves(value, high):
    value = value.reshape((value.shape[0] // 2, 2) + value.shape[1:])
    even, odd = value[:, 0], value[:, 1]
    return jnp.where(high, odd, even), jnp.where(high, even, odd)


def join_coefficients(sizes, axis, buffer, cyclic):
    me = lax.axis_index(axis)
    chain = [buffer[:, i] for i in range(5)]
    steps = []
    for level in range(sizes[axis].bit_length() - 1):
        high = (me // (1 << level)) % 2 == 1
        pairs = [halves(value, high) for value in chain]
        chain, inverse = merge([a for a, b in pairs], [b for a, b in pairs])
        steps.append((high, inverse, middle([value[0] for value in inverse], high)))
    coupling, e_first, e_last, k_first, k_last = [value[0] for value in chain]
    if cyclic:
        coupling = coupling + HALF * (k_last + k_first)
    inverse = 1.0 / (e_first * e_last + coupling * (e_first + e_last))
    closing = (
        (e_last + coupling) * inverse,
        coupling * inverse,
        (e_first + coupling) * inverse,
    )
    return steps, closing


def find_ends(joined, buffer, ends):
    steps, closing = joined
    count = ends.shape[0] // 2
    first, last = buffer[:, 0:count], buffer[:, count : 2 * count]
    inner_parts = []
    for high, inverse, weights in steps:
        f_l, f_r = halves(first, high)
        l_l, l_r = halves(last, high)
        first, last, u, v = join_right([value[:, None] for value in inverse], f_l, l_l, f_r, l_r)
        inner_parts.append(jnp.where(high, v[0], u[0]))
    first, last = first[0], last[0]
    first, last = (
        closing[0] * first + closing[1] * last,
        closing[1] * first + closing[2] * last,
    )
    for (high, inverse, weights), inner in reversed(list(zip(steps, inner_parts))):
        inner = inner + weights[0] * first + weights[1] * last
        first = jnp.where(high, inner, first)
        last = jnp.where(high, last, inner)
    ends[0:count] = first
    ends[count : 2 * count] = last


def kernel(sizes, parts, tracers_hbm, kappa_hbm, out_ref, *scratch):
    pieces = len(parts)
    tracers_ref, kappa_ref, x_field, x_kappa = scratch[:4]
    scratch = scratch[4:]
    x_cells, x_levels, x_kept, x_kept_levels, x_coef = scratch[:5]
    x_buffers, x_ends = scratch[5 : 5 + pieces], scratch[5 + pieces : 5 + 2 * pieces]
    scratch = scratch[5 + 2 * pieces :]
    y_cells, y_levels, y_kept, y_kept_levels, y_coef = scratch[:5]
    y_buffers, y_ends = scratch[5 : 5 + pieces], scratch[5 + pieces : 5 + 2 * pieces]
    x_send, x_recv, y_send, y_recv, in_sems = scratch[5 + 2 * pieces :]
    tracers, planes, rows, columns = tracers_ref.shape
    y_parts = [(2 * start, 2 * count) for start, count in parts]

    barrier = pltpu.get_barrier_semaphore()
    partners = 0
    for axis in sizes:
        for bits in reversed(range(1, sizes[axis])):
            pl.semaphore_signal(
                barrier,
                inc=1,
                device_id=device(sizes, axis, bits),
                device_id_type=pl.DeviceIdType.MESH,
            )
            partners += 1
    kappa_copy = pltpu.make_async_copy(kappa_hbm, kappa_ref, in_sems.at[pieces])
    kappa_copy.start()
    loads = []
    for piece, (start, count) in enumerate(y_parts):
        block = pl.ds(start, count)
        load = pltpu.make_async_copy(
            tracers_hbm.at[block], tracers_ref.at[block], in_sems.at[piece]
        )
        load.start()
        loads.append(load)

    kappa_copy.wait()
    for plane in range(planes):
        block = kappa_ref[plane]
        x_kappa[plane] = jnp.concatenate([block, block], 0).T
    factor(x_kappa, x_cells, x_levels, x_coef)

    faces = [0.5 * RATE_Z * (kappa_ref[z] + kappa_ref[z + 1]) for z in range(planes - 1)]

    def load_pair(pair, carry):
        fields = [
            tracers_ref[pl.ds(2 * pair, 2), z].reshape(2 * rows, columns) for z in range(planes)
        ]
        flux = [
            jnp.concatenate([faces[z], faces[z]], 0) * (fields[z + 1] - fields[z])
            for z in range(planes - 1)
        ]
        for z in range(planes):
            start = fields[z]
            if z < planes - 1:
                start = start + flux[z]
            if z > 0:
                start = start - flux[z - 1]
            x_field[pair, z] = start.T
        return carry

    x_copies = []
    for piece, (start, count) in enumerate(parts):
        loads[piece].wait()
        lax.fori_loop(start, start + count, load_pair, 0)
        for plane in range(planes):
            eliminate(
                x_field,
                parts[piece],
                plane,
                x_cells,
                x_levels,
                x_kept,
                x_kept_levels,
                x_buffers[piece],
            )
        if piece == 0:
            pl.semaphore_wait(barrier, partners)
            x_copies.append(send(sizes, "gx", x_coef, x_send, x_recv, pieces))
        x_copies.append(send(sizes, "gx", x_buffers[piece], x_send, x_recv, piece))
    factor(kappa_ref, y_cells, y_levels, y_coef)
    y_copies = [send(sizes, "gy", y_coef, y_send, y_recv, pieces)]
    for copy in x_copies[0]:
        copy.wait()
    x_joined = join_coefficients(sizes, "gx", x_coef, True)

    def turn_pair(pair, carry):
        for z in range(planes):
            out_ref[pl.ds(2 * pair, 2), z] = x_field[pair, z].T.reshape(2, rows, columns)
        return carry

    for piece, (start, count) in enumerate(parts):
        for copy in x_copies[piece + 1]:
            copy.wait()
        find_ends(x_joined, x_buffers[piece], x_ends[piece])
        for plane in range(planes):
            back(
                x_field,
                parts[piece],
                plane,
                x_cells,
                x_levels,
                x_kept,
                x_kept_levels,
                x_ends[piece],
            )
        lax.fori_loop(start, start + count, turn_pair, 0)
        for plane in range(planes):
            eliminate(
                out_ref,
                y_parts[piece],
                plane,
                y_cells,
                y_levels,
                y_kept,
                y_kept_levels,
                y_buffers[piece],
            )
        y_copies.append(send(sizes, "gy", y_buffers[piece], y_send, y_recv, piece))
    for copy in y_copies[0]:
        copy.wait()
    y_joined = join_coefficients(sizes, "gy", y_coef, False)
    for piece in range(pieces):
        for copy in y_copies[piece + 1]:
            copy.wait()
        find_ends(y_joined, y_buffers[piece], y_ends[piece])
        for plane in range(planes):
            back(
                out_ref,
                y_parts[piece],
                plane,
                y_cells,
                y_levels,
                y_kept,
                y_kept_levels,
                y_ends[piece],
            )


def shards(sizes, tracers, kappa):
    count, planes, rows, columns = tracers.shape
    pairs = count // 2
    lanes = 2 * rows
    parts = [(0, 1)] + [(start, min(2, pairs - start)) for start in range(1, pairs, 2)]

    def scratch(*shape):
        return pltpu.VMEM(shape, jnp.float32)

    def line(each, length, width, axis):
        fields = each * pairs
        group = length // SUB
        size = sizes[axis]
        return (
            [
                scratch(group, 3, planes, SUB, width),
                scratch(3, 7, planes, SUB, width),
                scratch(group, fields, planes, SUB, width),
                scratch(3, fields, planes, SUB, width),
                scratch(size, 5, planes, width),
            ]
            + [scratch(size, 2 * each * number, planes, width) for _, number in parts]
            + [scratch(2 * each * number, planes, width) for _, number in parts]
        )

    semaphores = [
        pltpu.SemaphoreType.DMA((len(parts) + 1, sizes[axis])) for axis in ("gx", "gx", "gy", "gy")
    ]
    return pl.pallas_call(
        functools.partial(kernel, sizes, parts),
        out_shape=jax.ShapeDtypeStruct(tracers.shape, jnp.float32),
        in_specs=[pl.BlockSpec(memory_space=pltpu.HBM)] * 2,
        out_specs=pl.BlockSpec(memory_space=pltpu.VMEM),
        scratch_shapes=[
            scratch(*tracers.shape),
            scratch(*kappa.shape),
            scratch(pairs, planes, columns, lanes),
            scratch(planes, columns, lanes),
        ]
        + line(1, columns, lanes, "gx")
        + line(2, rows, columns, "gy")
        + semaphores
        + [pltpu.SemaphoreType.DMA((len(parts) + 1,))],
        compiler_params=pltpu.CompilerParams(
            collective_id=0, has_side_effects=True, vmem_limit_bytes=52 * 1024 * 1024
        ),
    )(tracers, kappa)


def solution(mesh):
    sizes = {name: mesh.shape[name] for name in ("gx", "gy")}
    placed = (P(None, None, "gy", "gx"), P(None, "gy", "gx"))
    return jax.shard_map(
        functools.partial(shards, sizes),
        mesh=mesh,
        in_specs=placed,
        out_specs=P(None, None, "gy", "gx"),
        check_vma=False,
    )
```
